32 devices in a mesh: frow: 8 (over z, x), fcol: 4 (over y, core).
Axes of the slice: x: 2, y: 2, z: 4, core: 2. Of those that a mesh axis runs over, the one named last changes fastest.
Arguments:
- sigma_anc: float32 [29952, 29952], P('frow', 'fcol'), may hold values from -6 to 6
- lower: float32 [29952, 512], P(('frow', 'fcol')), may hold values from -0.5547002 to 0.5547002
- inv_diag: float32 [2, 256, 256], replicated, may hold values from -1.2 to 1.2
- sep_lower: float32 [512, 512], replicated, may hold values from -0.375 to 0.375
- row_pattern: int32 [2, 32], P(None, ('frow', 'fcol')), may hold values 0 or 1
Outputs:
- off_rows: float32 [29952, 512], P(('frow', 'fcol'))
- sep_sigma: float32 [512, 512], replicated
The draws below stay inside these ranges and needn't reach their ends.
All inputs are finite; a program needn't handle non-finite values. No bound on the sum of `row_pattern` on one device may be relied on, other than what follows from the above.
Results may differ from the reference program's by a relative error of at most 0.00011.
Values sent between devices are 32-bit elements; how exact they have to be, the bound alone decides.
No kernel may reach another device: no remote copies, remote signals or barrier semaphores. Data moves between devices by JAX's collectives and lax.ppermute only.
A program may use at most 192 MiB of HBM per device.

```python
import math
import jax
import jax.numpy as jnp
from jax import lax

B = 256
PANELS = 2
NR = 29952
BLOCKS = 32
N_FROW = 8
N_FCOL = 4


def draw_inv_diag(key, part):
    key = jax.random.fold_in(key, 11)
    sign_key, size_key, off_key = jax.random.split(key, 3)
    spread = 0.3 / math.sqrt(B)
    off_part = spread * jnp.clip(jax.random.normal(off_key, (PANELS, B, B), jnp.float32), -4.0, 4.0)
    magnitude = jax.random.uniform(size_key, (PANELS, B), jnp.float32, 0.8, 1.2)
    signs = jnp.where(jax.random.bernoulli(sign_key, 0.5, (PANELS, B)), 1.0, -1.0).astype(jnp.float32)
    identity = jnp.eye(B, dtype=jnp.float32)
    return off_part * (1.0 - identity) + (signs * magnitude)[:, :, None] * identity


def with_ends(entries, rng, smallest, largest):
    shape = entries.shape
    place = [jax.random.randint(jax.random.fold_in(rng, axis), (), 0, shape[axis]) for axis in range(len(shape))]
    entries = entries.at[tuple(place)].set(smallest)
    longest = shape.index(max(shape))
    place[longest] = (place[longest] + 1) % shape[longest]
    return entries.at[tuple(place)].set(largest)


def block_scale(key, dims, cuts, least, top_value):
    def one(dim, parts):
        draws = jax.random.uniform(jax.random.fold_in(jax.random.fold_in(key, 6), dim), (parts,), jnp.float32, least / len(cuts), top_value / len(cuts))
        return jnp.repeat(jnp.exp(draws), dims[dim] // parts).reshape((-1,) + (1,) * (len(dims) - dim - 1))

    gain = one(*cuts[0])
    for cut in cuts[1:]:
        gain = gain * one(*cut)
    return gain


def centred(stream_key, dims, scale, limit, cuts=(), kind=jnp.bfloat16):
    entries = scale * jax.random.normal(stream_key, dims, jnp.float32)
    if cuts:
        entries = entries * block_scale(stream_key, dims, cuts, -0.22, 0.18)
    return jnp.clip(entries, -limit, limit).astype(kind)


def setup_inputs(seed: int = 0) -> dict:
    seeds = jax.random.split(jax.random.key(seed), 6)
    return {
        "sigma_anc": centred(seeds[0], (NR, NR), 1.0, 6.0, ((0, 8), (1, 4)), jnp.float32),
        "lower": centred(seeds[1], (NR, PANELS * B), (4 * (NR // 16) ** -0.5), 0.5547002, ((0, 32),), jnp.float32),
        "inv_diag": draw_inv_diag(jax.random.fold_in(seeds[5], 71), 0),
        "sep_lower": centred(seeds[3], (PANELS * B, PANELS * B), B ** -0.5, 0.375, (), jnp.float32),
        "row_pattern": with_ends((jax.random.randint(seeds[4], (PANELS, BLOCKS), 0, 4) < 3).astype(jnp.int32), jax.random.fold_in(seeds[4], 1), 0, 1),
    }


def matmul(left_arg, right_arg):
    return jnp.dot(left_arg, right_arg, precision=lax.Precision.HIGHEST, preferred_element_type=jnp.float32)


def crossed(left_arg, right_arg):
    return matmul(left_arg.T, right_arg)


def reference(sigma_anc, lower, inv_diag, sep_lower, row_pattern):
    row_block = NR // (N_FROW * N_FCOL)
    tri_inv = jnp.tril(inv_diag)
    row_mask = jnp.repeat(row_pattern.astype(jnp.float32), row_block, axis=1)
    weighted = [matmul(lower[:, column * B:(column + 1) * B] * row_mask[column][:, None], tri_inv[column]) for column in range(PANELS)]
    stacked = jnp.concatenate(weighted, axis=1)
    permuted = stacked.reshape(N_FROW, N_FCOL, row_block, PANELS * B).transpose(1, 0, 2, 3).reshape(NR, PANELS * B)
    applied = matmul(sigma_anc, permuted)
    coupled = {}
    for current in range(PANELS):
        for later in range(current + 1, PANELS):
            coupled[(later, current)] = matmul(sep_lower[later * B:(later + 1) * B, current * B:(current + 1) * B], tri_inv[current])
    rows_sig = {}
    cross = {}
    diag = {}

    def sep_block(first, second):
        if first == second:
            return diag[first]
        if second > first:
            return cross[(second, first)].T
        return cross[(first, second)]

    for current in reversed(range(PANELS)):
        later_set = list(range(current + 1, PANELS))
        block_rows = -applied[:, current * B:(current + 1) * B]
        for later in later_set:
            block_rows = block_rows - matmul(rows_sig[later], coupled[(later, current)])
        rows_sig[current] = block_rows
        for later in later_set:
            entry = -crossed(rows_sig[later], weighted[current])
            for third in later_set:
                entry = entry - matmul(sep_block(later, third), coupled[(third, current)])
            cross[(later, current)] = entry
        inner = crossed(tri_inv[current], tri_inv[current]) - crossed(block_rows, weighted[current])
        for later in later_set:
            inner = inner - crossed(coupled[(later, current)], cross[(later, current)])
        diag[current] = inner
    off_rows = jnp.concatenate([rows_sig[column] for column in range(PANELS)], axis=1)
    sep_sigma = jnp.concatenate([jnp.concatenate([sep_block(first, second) for second in range(PANELS)], axis=1) for first in range(PANELS)], axis=0)
    return off_rows, sep_sigma
```

```python
import functools
import math

import jax
import jax.numpy as jnp
import numpy as np
from jax import lax
from jax.experimental import pallas as pl
from jax.experimental.pallas import tpu as pltpu
from jax.sharding import PartitionSpec as P

LANES = 128
SIDES = 2
LONGEST_LINE = 4


def matmul(left_arg, right_arg):
    return jnp.dot(
        left_arg, right_arg, precision=lax.Precision.HIGH, preferred_element_type=jnp.float32
    )


def crossed(left_arg, right_arg):
    return lax.dot_general(
        left_arg,
        right_arg,
        (((0,), (0,)), ((), ())),
        precision=lax.Precision.HIGH,
        preferred_element_type=jnp.float32,
    )


def two_parts(values):
    high = values.astype(jnp.bfloat16)
    return high, (values - high.astype(jnp.float32)).astype(jnp.bfloat16)


def window_kernel(windows, has_sum, places, s_main, s_last, *refs):
    items = refs[: 2 * windows]
    refs = refs[2 * windows :]
    sum_in = None
    if has_sum:
        sum_in, refs = refs[0], refs[1:]
    out, w_rows, w_high, w_low, s_high, s_low = refs
    row_step = pl.program_id(0)
    window = pl.program_id(1)
    depth = w_rows.shape[0]
    main = s_main.shape[1]
    count = items[0].shape[0]
    side = places[4 * windows]

    for place in range(windows):
        valid = places[4 * place + 2] > 0

        @pl.when((row_step == 0) & (window == place) & valid)
        def _():
            offset = places[4 * place + 1]
            w_rows[:LANES, :] = jnp.zeros((LANES, w_rows.shape[1]), jnp.float32)
            tail = 2 * count
            w_rows[tail:, :] = jnp.zeros((depth - tail, w_rows.shape[1]), jnp.float32)
            mine = pl.multiple_of(offset + side * count, 8)
            other = pl.multiple_of(offset + (1 - side) * count, 8)
            w_rows[pl.ds(mine, count), :] = items[2 * place][...]
            w_rows[pl.ds(other, count), :] = items[2 * place + 1][...]
            high, low = two_parts(w_rows[...])
            w_high[place] = high
            w_low[place] = low

    @pl.when(window == 0)
    def _():
        if has_sum:
            out[...] = sum_in[...]
        else:
            out[...] = jnp.zeros_like(out)

    @pl.when(places[4 * window + 2] > 0)
    def _():
        high, low = two_parts(s_main[...])
        s_high[:, :main] = high
        s_low[:, :main] = low
        lane = lax.broadcasted_iota(jnp.int32, s_last.shape, 1)
        last = jnp.where(lane < places[4 * window + 3], s_last[...], 0.0)
        high, low = two_parts(last)
        s_high[:, main:] = high
        s_low[:, main:] = low
        total = jnp.dot(s_high[...], w_high[window], preferred_element_type=jnp.float32)
        total += jnp.dot(s_high[...], w_low[window], preferred_element_type=jnp.float32)
        total += jnp.dot(s_low[...], w_high[window], preferred_element_type=jnp.float32)
        out[...] += total


def row_tile(rows):
    best = 8
    for tile in range(16, min(rows, 640) + 1, 16):
        if rows % tile == 0:
            best = tile
    return best


def window_shape(pair, line):
    depth = 0
    for place in range(line):
        depth = max(depth, (pair * place) % LANES + pair)
    return -(-depth // (2 * LANES)) * (2 * LANES)


def line_tables(steps, pair, line, depth, columns):
    main = depth - LANES
    rows = []
    for index in range(line * SIDES):
        here, side = divmod(index, SIDES)
        found = [here + step for step in steps]
        valids = [int(0 <= at < line) for at in found]
        starts = [pair * min(max(at, 0), line - 1) for at in found]
        bases = [start // LANES for start in starts]
        shared = max([base * valid for base, valid in zip(bases, valids)])
        row = []
        for start, base, valid in zip(starts, bases, valids):
            used = base if valid else shared
            row += [used, start % LANES, valid, columns - used * LANES - main]
        rows.append(row + [side, max(valids)])
    return np.asarray(rows, np.int32)


def at_index(table, axis):
    return lax.dynamic_index_in_dim(jnp.asarray(table), lax.axis_index(axis), 0, keepdims=False)


def add_windows(sigma, items, line_steps, total, line):
    rows, columns = sigma.shape
    count, width = items[0].shape
    pair = 2 * count
    windows = len(line_steps)
    depth = window_shape(pair, line)
    main = depth - LANES
    tile = row_tile(rows)
    steps = rows // tile
    places = at_index(line_tables(line_steps, pair, line, depth, columns), "frow")

    def s_main_at(row_step, window, places):
        return (
            pl.multiple_of(row_step * places[4 * windows + 1] * tile, tile),
            pl.multiple_of(places[4 * window] * LANES, LANES),
        )

    def s_last_at(row_step, window, places):
        return (row_step * places[4 * windows + 1], places[4 * window] + main // LANES)

    def rows_at(row_step, window, places):
        return (row_step * places[4 * windows + 1], 0)

    def whole(row_step, window, places):
        return (0, 0)

    in_specs = [
        pl.BlockSpec((pl.Element(tile), pl.Element(main)), s_main_at),
        pl.BlockSpec((tile, LANES), s_last_at),
    ]
    in_specs += [pl.BlockSpec((count, width), whole)] * len(items)
    operands = [places, sigma, sigma] + list(items)
    aliases = {}
    if total is not None:
        in_specs.append(pl.BlockSpec((tile, width), rows_at))
        aliases = {len(operands): 0}
        operands.append(total)
    return pl.pallas_call(
        functools.partial(window_kernel, windows, total is not None),
        out_shape=jax.ShapeDtypeStruct((rows, width), jnp.float32),
        grid_spec=pltpu.PrefetchScalarGridSpec(
            num_scalar_prefetch=1,
            grid=(steps, windows),
            in_specs=in_specs,
            out_specs=pl.BlockSpec((tile, width), rows_at),
            scratch_shapes=[
                pltpu.VMEM((depth, width), jnp.float32),
                pltpu.VMEM((windows, depth, width), jnp.bfloat16),
                pltpu.VMEM((windows, depth, width), jnp.bfloat16),
                pltpu.VMEM((tile, depth), jnp.bfloat16),
                pltpu.VMEM((tile, depth), jnp.bfloat16),
            ],
        ),
        input_output_aliases=aliases,
        compiler_params=pltpu.CompilerParams(
            dimension_semantics=("arbitrary", "arbitrary"), vmem_limit_bytes=48 * 1024 * 1024
        ),
        cost_estimate=pl.CostEstimate(
            flops=6 * rows * depth * width, bytes_accessed=4 * rows * depth, transcendentals=0
        ),
    )(*operands)


def ring(size, step):
    return [(index, (index + step) % size) for index in range(size)]


def turned(stack, start, piece):
    return lax.dynamic_slice_in_dim(
        jnp.concatenate([stack, stack], axis=0), start * piece, stack.shape[0], axis=0
    )


def sum_piece(values, axis, size):
    piece = values.shape[0] // size
    ordered = turned(values, lax.axis_index(axis), piece)
    total = ordered[:piece]
    for step in range(1, size):
        total = total + lax.ppermute(
            ordered[step * piece : (step + 1) * piece], axis, ring(size, step)
        )
    return total


def join_pieces(piece, axis, size):
    parts = [piece] + [lax.ppermute(piece, axis, ring(size, -step)) for step in range(1, size)]
    back = at_index(np.asarray([-index % size for index in range(size)], np.int32), axis)
    return turned(jnp.concatenate(parts, axis=0), back, piece.shape[0])


def sum_everywhere(values, n_frow, n_fcol):
    part = sum_piece(values, "fcol", n_fcol)
    part = sum_piece(part, "frow", n_frow)
    part = join_pieces(part, "frow", n_frow)
    return join_pieces(part, "fcol", n_fcol)


def scatter_rows(partial, n_fcol):
    fars = n_fcol // 2
    count = partial.shape[0] // n_fcol
    swap_near = [(i, i ^ 1) for i in range(n_fcol)]
    table = [
        [(i // 2 + step) % fars * 2 + near for step in range(1, fars + 1) for near in (i % 2, 1 - i % 2)]
        for i in range(n_fcol)
    ]
    starts = at_index(np.asarray(table, np.int32) * count, "fcol")

    def block(which):
        return lax.dynamic_slice_in_dim(partial, starts[which], count, axis=0)

    halves = [
        block(2 * step) + lax.ppermute(block(2 * step + 1), "fcol", swap_near)
        for step in range(fars)
    ]
    total = halves[-1]
    for step in range(1, fars):
        perm = [(i, (i + 2 * step) % n_fcol) for i in range(n_fcol)]
        total = total + lax.ppermute(halves[step - 1], "fcol", perm)
    return total


def apply_sigma(sigma, weighted, line, order):
    def along(step):
        return [
            (z * SIDES + x, (z + step) * SIDES + x)
            for z in range(line)
            for x in range(SIDES)
            if 0 <= z + step < line
        ]

    def across(places):
        return [(z * SIDES + x, z * SIDES + 1 - x) for z in places for x in range(SIDES)]

    def send(values, perm):
        return lax.ppermute(values, "frow", perm)

    applied = {}
    for column in order:
        own = weighted[column]
        groups = [([own, send(own, across(range(line)))], [0])]
        up = down = own
        for step in range(1, line):
            up = send(up, along(1))
            down = send(down, along(-1))
            items = [
                down,
                send(down, across(range(line - step))),
                up,
                send(up, across(range(step, line))),
            ]
            groups.append((items, [step, -step]))
        total = None
        for items, steps in groups:
            total = add_windows(sigma, items, steps, total, line)
        applied[column] = total
    return applied


def on_device(n_frow, n_fcol, sigma_anc, lower, inv_diag, sep_lower, row_pattern):
    panels = inv_diag.shape[0]
    width = inv_diag.shape[1]
    tri_inv = jnp.tril(inv_diag)
    row_mask = row_pattern.astype(jnp.float32)
    order = list(reversed(range(panels)))
    count = lower.shape[0]
    short_line = n_frow % SIDES == 0 and n_frow // SIDES <= LONGEST_LINE
    by_line = short_line and count % 8 == 0 and n_fcol % 2 == 0 and width % LANES == 0
    by_line = by_line and width % (8 * n_frow * n_fcol) == 0
    weighted = {}
    for column in order:
        scaled = lower[:, column * width : (column + 1) * width] * row_mask[column, 0]
        weighted[column] = matmul(scaled, tri_inv[column])
    coupled = {}
    for current in range(panels):
        for later in range(current + 1, panels):
            coupled[later, current] = matmul(
                sep_lower[
                    later * width : (later + 1) * width, current * width : (current + 1) * width
                ],
                tri_inv[current],
            )
    if by_line:
        partial = apply_sigma(sigma_anc, weighted, n_frow // SIDES, order)
        applied = {column: scatter_rows(partial[column], n_fcol) for column in order}
    else:
        applied = {}
        for column in order:
            gathered = lax.all_gather(weighted[column], "frow", axis=0, tiled=True)
            applied[column] = lax.psum_scatter(
                matmul(sigma_anc, gathered), "fcol", scatter_dimension=0, tiled=True
            )
    rows_sig, products, cross, diag = {}, {}, {}, {}

    def sep_block(first, second):
        if first == second:
            return diag[first]
        if second > first:
            return cross[second, first].T
        return cross[first, second]

    for current in order:
        block_rows = -applied[current]
        for later in range(current + 1, panels):
            block_rows = block_rows - matmul(rows_sig[later], coupled[later, current])
        rows_sig[current] = block_rows
        earlier = jnp.concatenate([weighted[column] for column in range(current + 1)], axis=1)
        inner = crossed(block_rows, earlier)
        if by_line:
            inner = sum_everywhere(inner, n_frow, n_fcol)
        else:
            inner = lax.psum(inner, ("frow", "fcol"))
        for column in range(current + 1):
            products[current, column] = inner[:, column * width : (column + 1) * width]
    for current in order:
        later_set = list(range(current + 1, panels))
        for later in later_set:
            entry = -products[later, current]
            for third in later_set:
                entry = entry - matmul(sep_block(later, third), coupled[third, current])
            cross[later, current] = entry
        inner = crossed(tri_inv[current], tri_inv[current]) - products[current, current]
        for later in later_set:
            inner = inner - crossed(coupled[later, current], cross[later, current])
        diag[current] = inner
    off_rows = jnp.concatenate([rows_sig[column] for column in range(panels)], axis=1)
    sep_sigma = jnp.concatenate(
        [
            jnp.concatenate([sep_block(first, second) for second in range(panels)], axis=1)
            for first in range(panels)
        ],
        axis=0,
    )
    return off_rows, sep_sigma


def solution(mesh):
    in_specs = (P("frow", "fcol"), P(("frow", "fcol"), None), P(), P(), P(None, ("frow", "fcol")))
    out_specs = (P(("frow", "fcol"), None), P())
    return jax.shard_map(
        functools.partial(on_device, mesh.shape["frow"], mesh.shape["fcol"]),
        mesh=mesh,
        in_specs=in_specs,
        out_specs=out_specs,
        check_vma=False,
    )
```

```python
import functools
import math

import jax
import jax.numpy as jnp
import numpy as np
from jax import lax
from jax.experimental import pallas as pl
from jax.experimental.pallas import tpu as pltpu
from jax.sharding import PartitionSpec as P

LANES = 128
LONGEST_RING = 8


def matmul(left_arg, right_arg):
    return jnp.dot(
        left_arg, right_arg, precision=lax.Precision.HIGH, preferred_element_type=jnp.float32
    )


def crossed(left_arg, right_arg):
    return lax.dot_general(
        left_arg,
        right_arg,
        (((0,), (0,)), ((), ())),
        precision=lax.Precision.HIGH,
        preferred_element_type=jnp.float32,
    )


def two_parts(values):
    high = values.astype(jnp.bfloat16)
    return high, (values - high.astype(jnp.float32)).astype(jnp.bfloat16)


def window_kernel(has_sum, strip, places, *refs):
    mains, lasts, items = refs[0:2], refs[2:4], refs[4:6]
    refs = refs[6:]
    sum_in = None
    if has_sum:
        sum_in, refs = refs[0], refs[1:]
    out, w_rows, w_high, w_low = refs
    depth = w_rows.shape[0]
    count = items[0].shape[0]

    @pl.when(pl.program_id(0) == 0)
    def _():
        for window in range(2):
            w_rows[...] = jnp.zeros_like(w_rows)
            offset = pl.multiple_of(places[4 * window + 2], 8)
            w_rows[pl.ds(offset, count), :] = items[window][...]
            high, low = two_parts(w_rows[...])
            w_high[window * depth : (window + 1) * depth, :] = high
            w_low[window * depth : (window + 1) * depth, :] = low

    lane = lax.broadcasted_iota(jnp.int32, (strip, LANES), 1)
    for start in range(0, out.shape[0], strip):
        rows = slice(start, start + strip)
        highs, lows = [], []
        for window in range(2):
            last = jnp.where(lane < places[4 * window + 3], lasts[window][rows, :], 0.0)
            for values in (mains[window][rows, :], last):
                high, low = two_parts(values)
                highs.append(high)
                lows.append(low)
        high = jnp.concatenate(highs, axis=1)
        low = jnp.concatenate(lows, axis=1)
        total = jnp.dot(high, w_high[...], preferred_element_type=jnp.float32)
        total += jnp.dot(high, w_low[...], preferred_element_type=jnp.float32)
        total += jnp.dot(low, w_high[...], preferred_element_type=jnp.float32)
        if has_sum:
            total += sum_in[rows, :]
        out[rows, :] = total


def row_tiles(rows):
    tiles = [tile for tile in range(16, min(rows, 640) + 1, 16) if rows % tile == 0]
    tile = max(tiles)
    strips = [strip for strip in range(16, min(tile, 256) + 1, 16) if tile % strip == 0]
    return tile, max(strips)


def window_plan(count, blocks, columns):
    main = -(-(count + 8) // LANES) * LANES
    starts = [min(count * block, columns - main) // LANES * LANES for block in range(blocks)]
    fits = all(
        count * block - start + count <= main + LANES for block, start in enumerate(starts)
    )
    return main, starts, fits and columns >= main and count % 8 == 0


def add_windows(sigma, items, owners, total):
    rows, columns = sigma.shape
    count, width = items[0].shape
    blocks = columns // count
    main, starts, _ = window_plan(count, blocks, columns)
    depth = main + LANES
    tile, strip = row_tiles(rows)
    final = (columns - 1) // LANES
    table = []
    for pair in owners:
        row = []
        for block in pair:
            after = (starts[block] + main) // LANES
            room = max(columns - after * LANES, 0)
            row += [starts[block] // LANES, min(after, final), count * block - starts[block], room]
        table.append(row)
    places = at_index(np.asarray(table, np.int32), "frow")

    def main_at(window):
        return lambda step, places: (
            pl.multiple_of(step * tile, tile),
            pl.multiple_of(places[4 * window] * LANES, LANES),
        )

    def last_at(window):
        return lambda step, places: (step, places[4 * window + 1])

    in_specs = [
        pl.BlockSpec((pl.Element(tile), pl.Element(main)), main_at(window)) for window in range(2)
    ]
    in_specs += [pl.BlockSpec((tile, LANES), last_at(window)) for window in range(2)]
    in_specs += [pl.BlockSpec((count, width), lambda step, places: (0, 0))] * 2
    operands = [places] + [sigma] * 4 + list(items)
    aliases = {}
    if total is not None:
        in_specs.append(pl.BlockSpec((tile, width), lambda step, places: (step, 0)))
        aliases = {len(operands): 0}
        operands.append(total)
    return pl.pallas_call(
        functools.partial(window_kernel, total is not None, strip),
        out_shape=jax.ShapeDtypeStruct((rows, width), jnp.float32),
        grid_spec=pltpu.PrefetchScalarGridSpec(
            num_scalar_prefetch=1,
            grid=(rows // tile,),
            in_specs=in_specs,
            out_specs=pl.BlockSpec((tile, width), lambda step, places: (step, 0)),
            scratch_shapes=[
                pltpu.VMEM((depth, width), jnp.float32),
                pltpu.VMEM((2 * depth, width), jnp.bfloat16),
                pltpu.VMEM((2 * depth, width), jnp.bfloat16),
            ],
        ),
        input_output_aliases=aliases,
        compiler_params=pltpu.CompilerParams(
            dimension_semantics=("arbitrary",), vmem_limit_bytes=48 * 1024 * 1024
        ),
        cost_estimate=pl.CostEstimate(
            flops=12 * rows * depth * width, bytes_accessed=8 * rows * depth, transcendentals=0
        ),
    )(*operands)


def at_index(table, axis):
    return lax.dynamic_index_in_dim(jnp.asarray(table), lax.axis_index(axis), 0, keepdims=False)


def after(values, *others):
    return lax.optimization_barrier((values,) + others)[0]


def swapped(values, axis, size, bit):
    return lax.ppermute(values, axis, [(index, index ^ bit) for index in range(size)])


def sum_everywhere(values, beside, n_frow, n_fcol):
    bits = [1 << power for power in range(n_fcol.bit_length() - 1)]
    index = lax.axis_index("fcol")
    for bit in bits:
        half = values.shape[0] // 2
        mine = ((index & bit) != 0).astype(jnp.int32)
        kept = lax.dynamic_slice_in_dim(values, mine * half, half, axis=0)
        sent = lax.dynamic_slice_in_dim(values, (1 - mine) * half, half, axis=0)
        values = kept + swapped(sent, "fcol", n_fcol, bit)
    for power in range(n_frow.bit_length() - 1):
        values = values + swapped(values, "frow", n_frow, 1 << power)
    values = after(values, beside)
    for bit in reversed(bits):
        other = swapped(values, "fcol", n_fcol, bit)
        upper = (index & bit) != 0
        values = jnp.concatenate(
            [jnp.where(upper, other, values), jnp.where(upper, values, other)], axis=0
        )
    return values


def near_sums(partial, n_fcol):
    fars = n_fcol // 2
    count = partial.shape[0] // n_fcol
    table = [
        [
            (i // 2 + step) % fars * 2 + near
            for step in range(1, fars + 1)
            for near in (i % 2, 1 - i % 2)
        ]
        for i in range(n_fcol)
    ]
    starts = at_index(np.asarray(table, np.int32) * count, "fcol")

    def block(which):
        return lax.dynamic_slice_in_dim(partial, starts[which], count, axis=0)

    sent = [block(2 * step + 1) for step in range(fars)]
    return sent, [block(2 * step) + swapped(sent[step], "fcol", n_fcol, 1) for step in range(fars)]


def far_sum(halves, n_fcol):
    total = halves[-1]
    for step in range(1, len(halves)):
        perm = [(i, (i + 2 * step) % n_fcol) for i in range(n_fcol)]
        total = total + lax.ppermute(halves[step - 1], "fcol", perm)
    return total


def ring_order(size):
    line = size // 2
    return [2 * z for z in range(line)] + [2 * z + 1 for z in reversed(range(line))]


def apply_sigma(sigma, weighted, row_block, size, n_fcol, order):
    ring = ring_order(size)
    spot = {index: place for place, index in enumerate(ring)}

    def send(values, step):
        perm = [(ring[place], ring[(place + step) % size]) for place in range(size)]
        return lax.ppermute(values, "frow", perm)

    def owner(step):
        return [ring[(spot[index] - step) % size] for index in range(size)]

    width = weighted[order[0]].shape[1]
    applied, inner_products = {}, {}
    last = {1: None, -1: None}
    finished = None
    for turn, column in enumerate(order):
        own = weighted[column]
        long_way = 1 if turn % 2 == 0 else -1
        lengths = {long_way: size // 2, -long_way: size // 2 - 1}
        come = {0: own}
        held = {}
        for way in (1, -1):
            held[way] = own if last[way] is None else after(own, last[way])
        for step in range(1, size // 2 + 1):
            for way in (long_way, -long_way):
                if step <= lengths[way]:
                    held[way] = send(held[way], way)
                    come[way * step] = held[way]
                    if step == lengths[way] - 1:
                        last[way] = held[way]
        total = None
        for step in range(1, size // 2 + 1):
            pair = (-long_way * (step - 1), long_way * step)
            owners = list(zip(owner(pair[0]), owner(pair[1])))
            items = [come[pair[0]], come[pair[1]]]
            if finished is not None and step == 2:
                done, values = finished
                _, halves = near_sums(values, n_fcol)
                inner = crossed(values, row_block[:, : (done + 1) * width])
                items[1] = after(items[1], inner, *halves)
                inner = lax.psum(inner, "fcol")
                inner_products[done] = lax.psum(inner, "frow")
            if finished is not None and step == 3:
                applied[done] = far_sum(halves, n_fcol)
                items[1] = after(items[1], applied[done])
            if finished is not None and step == 4:
                items[1] = after(items[1], inner)
            total = add_windows(sigma, items, owners, total)
        finished = (column, total)
    done, values = finished
    sent, halves = near_sums(values, n_fcol)
    inner = crossed(after(values, *sent), row_block[:, : (done + 1) * width])
    applied[done] = far_sum(halves, n_fcol)
    inner_products[done] = sum_everywhere(after(inner, *halves), applied[done], size, n_fcol)
    return applied, inner_products


def on_device(n_frow, n_fcol, sigma_anc, lower, inv_diag, sep_lower, row_pattern):
    panels = inv_diag.shape[0]
    width = inv_diag.shape[1]
    tri_inv = jnp.tril(inv_diag)
    row_mask = row_pattern.astype(jnp.float32)
    order = list(reversed(range(panels)))
    count = lower.shape[0]
    by_ring = (
        n_frow in (4, LONGEST_RING)
        and n_fcol & (n_fcol - 1) == 0
        and width % (8 * n_fcol) == 0
        and width % LANES == 0
        and sigma_anc.shape[0] % 16 == 0
        and window_plan(count, n_frow, sigma_anc.shape[1])[2]
    )
    weighted = {}
    for column in order:
        scaled = lower[:, column * width : (column + 1) * width] * row_mask[column, 0]
        weighted[column] = matmul(scaled, tri_inv[column])
    coupled = {}
    for current in range(panels):
        for later in range(current + 1, panels):
            coupled[later, current] = matmul(
                sep_lower[
                    later * width : (later + 1) * width, current * width : (current + 1) * width
                ],
                tri_inv[current],
            )
    applied, inner_products = {}, {}
    if by_ring:
        by_columns = jnp.concatenate([weighted[column] for column in range(panels)], axis=1)
        row_block = lax.all_gather(by_columns, "fcol", axis=0, tiled=True)
        applied, inner_products = apply_sigma(
            sigma_anc, weighted, row_block, n_frow, n_fcol, order
        )
    else:
        for column in order:
            gathered = lax.all_gather(weighted[column], "frow", axis=0, tiled=True)
            applied[column] = lax.psum_scatter(
                matmul(sigma_anc, gathered), "fcol", scatter_dimension=0, tiled=True
            )
            inner_products[column] = lax.psum(
                crossed(
                    applied[column],
                    jnp.concatenate([weighted[k] for k in range(column + 1)], axis=1),
                ),
                ("frow", "fcol"),
            )
    rows_sig, products, cross, diag = {}, {}, {}, {}

    def sep_block(first, second):
        if first == second:
            return diag[first]
        if second > first:
            return cross[second, first].T
        return cross[first, second]

    for current in order:
        block_rows = -applied[current]
        for later in range(current + 1, panels):
            block_rows = block_rows - matmul(rows_sig[later], coupled[later, current])
        rows_sig[current] = block_rows
        for column in range(current + 1):
            inner = inner_products[current][:, column * width : (column + 1) * width]
            for later in range(current + 1, panels):
                inner = inner + crossed(coupled[later, current], products[later, column])
            products[current, column] = -inner
    for current in order:
        later_set = list(range(current + 1, panels))
        for later in later_set:
            entry = -products[later, current]
            for third in later_set:
                entry = entry - matmul(sep_block(later, third), coupled[third, current])
            cross[later, current] = entry
        inner = crossed(tri_inv[current], tri_inv[current]) - products[current, current]
        for later in later_set:
            inner = inner - crossed(coupled[later, current], cross[later, current])
        diag[current] = inner
    off_rows = jnp.concatenate([rows_sig[column] for column in range(panels)], axis=1)
    sep_sigma = jnp.concatenate(
        [
            jnp.concatenate([sep_block(first, second) for second in range(panels)], axis=1)
            for first in range(panels)
        ],
        axis=0,
    )
    return off_rows, sep_sigma


def solution(mesh):
    in_specs = (P("frow", "fcol"), P(("frow", "fcol"), None), P(), P(), P(None, ("frow", "fcol")))
    out_specs = (P(("frow", "fcol"), None), P())
    return jax.shard_map(
        functools.partial(on_device, mesh.shape["frow"], mesh.shape["fcol"]),
        mesh=mesh,
        in_specs=in_specs,
        out_specs=out_specs,
        check_vma=False,
    )
```

```python
import functools
import math

import jax
import jax.numpy as jnp
import numpy as np
from jax import lax
from jax.experimental import pallas as pl
from jax.experimental.pallas import tpu as pltpu
from jax.sharding import PartitionSpec as P

LANES = 128
LONGEST_RING = 8


def matmul(left_arg, right_arg):
    return jnp.dot(
        left_arg, right_arg, precision=lax.Precision.HIGH, preferred_element_type=jnp.float32
    )


def crossed(left_arg, right_arg):
    return lax.dot_general(
        left_arg,
        right_arg,
        (((0,), (0,)), ((), ())),
        precision=lax.Precision.HIGH,
        preferred_element_type=jnp.float32,
    )


def two_parts(values):
    high = values.astype(jnp.bfloat16)
    return high, (values - high.astype(jnp.float32)).astype(jnp.bfloat16)


def product(left_parts, right_parts, dims=(((1,), (0,)), ((), ()))):
    def one(left, right):
        return lax.dot_general(left, right, dims, preferred_element_type=jnp.float32)

    (high, low), (other_high, other_low) = left_parts, right_parts
    return one(high, other_high) + one(high, other_low) + one(low, other_high)


def weights_kernel(pattern, lower, inv_diag, out):
    width = inv_diag.shape[1]
    below = lax.broadcasted_iota(jnp.int32, (width, width), 0) >= lax.broadcasted_iota(
        jnp.int32, (width, width), 1
    )
    for panel in range(inv_diag.shape[0]):
        columns = slice(panel * width, (panel + 1) * width)
        scaled = lower[:, columns] * pattern[panel, 0].astype(jnp.float32)
        tri_inv = jnp.where(below, inv_diag[panel], 0.0)
        out[:, columns] = product(two_parts(scaled), two_parts(tri_inv))


def all_weights(lower, inv_diag, row_pattern):
    return pl.pallas_call(
        weights_kernel,
        out_shape=jax.ShapeDtypeStruct(lower.shape, jnp.float32),
        in_specs=[
            pl.BlockSpec(memory_space=pltpu.SMEM),
            pl.BlockSpec(memory_space=pltpu.VMEM),
            pl.BlockSpec(memory_space=pltpu.VMEM),
        ],
        out_specs=pl.BlockSpec(memory_space=pltpu.VMEM),
        compiler_params=pltpu.CompilerParams(vmem_limit_bytes=32 * 1024 * 1024),
    )(row_pattern, lower, inv_diag)


def window_kernel(plan, places, *refs):
    windows, parts, has_sum, with_inner, panels, strip = plan
    refs = list(refs)
    mains = [refs.pop(0) for _ in range(windows)]
    lasts = [refs.pop(0) for _ in range(windows)]
    items = [[refs.pop(0) for _ in range(parts)] for _ in range(windows)]
    sum_in = refs.pop(0) if has_sum else None
    row_block = refs.pop(0) if with_inner else None
    out = refs.pop(0)
    inner = refs.pop(0) if with_inner else None
    w_rows, w_high, w_low = refs
    depth = w_rows.shape[0]
    count, part_width = items[0][0].shape

    @pl.when(pl.program_id(0) == 0)
    def _():
        for window in range(windows):
            w_rows[...] = jnp.zeros_like(w_rows)
            offset = pl.multiple_of(places[4 * window + 2], 8)
            for part in range(parts):
                columns = slice(part * part_width, (part + 1) * part_width)
                w_rows[pl.ds(offset, count), columns] = items[window][part][...]
            high, low = two_parts(w_rows[...])
            w_high[window * depth : (window + 1) * depth, :] = high
            w_low[window * depth : (window + 1) * depth, :] = low
        if with_inner:
            inner[...] = jnp.zeros_like(inner)

    lane = lax.broadcasted_iota(jnp.int32, (strip, LANES), 1)
    for start in range(0, out.shape[0], strip):
        rows = slice(start, start + strip)
        highs, lows = [], []
        for window in range(windows):
            last = jnp.where(lane < places[4 * window + 3], lasts[window][rows, :], 0.0)
            for values in (mains[window][rows, :], last):
                high, low = two_parts(values)
                highs.append(high)
                lows.append(low)
        high = jnp.concatenate(highs, axis=1)
        low = jnp.concatenate(lows, axis=1)
        total = product((high, low), (w_high[...], w_low[...]))
        if has_sum:
            total += sum_in[rows, :]
        out[rows, :] = total
        if with_inner:
            width = total.shape[1] // panels
            others = two_parts(row_block[rows, :])
            at = 0
            for panel in range(panels):
                mine = two_parts(total[:, panel * width : (panel + 1) * width])
                upto = (panel + 1) * width
                inner[:, at : at + upto] += product(
                    mine, [other[:, :upto] for other in others], (((0,), (0,)), ((), ()))
                )
                at += upto


def row_tiles(rows):
    tiles = [tile for tile in range(16, min(rows, 640) + 1, 16) if rows % tile == 0]
    tile = max(tiles)
    strips = [strip for strip in range(16, min(tile, 256) + 1, 16) if tile % strip == 0]
    return tile, max(strips)


def window_plan(count, blocks, columns):
    main = -(-(count + 8) // LANES) * LANES
    starts = [min(count * block, columns - main) // LANES * LANES for block in range(blocks)]
    fits = all(
        count * block - start + count <= main + LANES for block, start in enumerate(starts)
    )
    return main, starts, fits and columns >= main and count % 8 == 0


def add_windows(sigma, items, owners, total, row_block=None, panels=1):
    rows, columns = sigma.shape
    count = items[0][0].shape[0]
    parts = len(items[0])
    width = parts * items[0][0].shape[1]
    windows = len(items)
    main, starts, _ = window_plan(count, columns // count, columns)
    depth = main + LANES
    tile, strip = row_tiles(rows)
    final = (columns - 1) // LANES
    table = []
    for blocks in owners:
        row = []
        for block in blocks:
            behind = (starts[block] + main) // LANES
            room = max(columns - behind * LANES, 0)
            row += [starts[block] // LANES, min(behind, final), count * block - starts[block], room]
        table.append(row)
    places = at_index(np.asarray(table, np.int32), "frow")

    def main_at(window):
        return lambda step, places: (
            pl.multiple_of(step * tile, tile),
            pl.multiple_of(places[4 * window] * LANES, LANES),
        )

    def last_at(window):
        return lambda step, places: (step, places[4 * window + 1])

    def by_row(step, places):
        return (step, 0)

    def whole(step, places):
        return (0, 0)

    in_specs = [
        pl.BlockSpec((pl.Element(tile), pl.Element(main)), main_at(k)) for k in range(windows)
    ]
    in_specs += [pl.BlockSpec((tile, LANES), last_at(k)) for k in range(windows)]
    in_specs += [pl.BlockSpec((count, width // parts), whole)] * (windows * parts)
    operands = [places] + [sigma] * (2 * windows) + [part for item in items for part in item]
    aliases = {}
    if total is not None:
        in_specs.append(pl.BlockSpec((tile, width), by_row))
        aliases = {len(operands): 0}
        operands.append(total)
    out_shape = [jax.ShapeDtypeStruct((rows, width), jnp.float32)]
    out_specs = [pl.BlockSpec((tile, width), by_row)]
    flops = 6 * rows * windows * depth * width
    if row_block is not None:
        in_specs.append(pl.BlockSpec((tile, width), by_row))
        operands.append(row_block)
        panel_width = width // panels
        inner_shape = (panel_width, panel_width * panels * (panels + 1) // 2)
        out_shape.append(jax.ShapeDtypeStruct(inner_shape, jnp.float32))
        out_specs.append(pl.BlockSpec(inner_shape, whole))
        flops += 6 * rows * inner_shape[0] * inner_shape[1]
    plan = (windows, parts, total is not None, row_block is not None, panels, strip)
    return pl.pallas_call(
        functools.partial(window_kernel, plan),
        out_shape=out_shape,
        grid_spec=pltpu.PrefetchScalarGridSpec(
            num_scalar_prefetch=1,
            grid=(rows // tile,),
            in_specs=in_specs,
            out_specs=out_specs,
            scratch_shapes=[
                pltpu.VMEM((depth, width), jnp.float32),
                pltpu.VMEM((windows * depth, width), jnp.bfloat16),
                pltpu.VMEM((windows * depth, width), jnp.bfloat16),
            ],
        ),
        input_output_aliases=aliases,
        compiler_params=pltpu.CompilerParams(
            dimension_semantics=("arbitrary",), vmem_limit_bytes=52 * 1024 * 1024
        ),
        cost_estimate=pl.CostEstimate(
            flops=flops, bytes_accessed=4 * rows * windows * depth, transcendentals=0
        ),
    )(*operands)


def at_index(table, axis):
    return lax.dynamic_index_in_dim(jnp.asarray(table), lax.axis_index(axis), 0, keepdims=False)


def after(values, *others):
    return lax.optimization_barrier((values,) + others)[0]


def swapped(values, axis, size, bit):
    return lax.ppermute(values, axis, [(index, index ^ bit) for index in range(size)])


def sum_everywhere(values, beside, n_frow, n_fcol):
    bits = [1 << power for power in range(n_fcol.bit_length() - 1)]
    index = lax.axis_index("fcol")
    for bit in bits:
        half = values.shape[0] // 2
        mine = ((index & bit) != 0).astype(jnp.int32)
        kept = lax.dynamic_slice_in_dim(values, mine * half, half, axis=0)
        sent = lax.dynamic_slice_in_dim(values, (1 - mine) * half, half, axis=0)
        values = kept + swapped(sent, "fcol", n_fcol, bit)
    for power in range(n_frow.bit_length() - 1):
        values = values + swapped(values, "frow", n_frow, 1 << power)
    values = after(values, beside)
    for bit in reversed(bits):
        other = swapped(values, "fcol", n_fcol, bit)
        upper = (index & bit) != 0
        values = jnp.concatenate(
            [jnp.where(upper, other, values), jnp.where(upper, values, other)], axis=0
        )
    return values


def near_sums(partial, n_fcol):
    fars = n_fcol // 2
    count = partial.shape[0] // n_fcol
    table = [
        [
            (i // 2 + step) % fars * 2 + near
            for step in range(1, fars + 1)
            for near in (i % 2, 1 - i % 2)
        ]
        for i in range(n_fcol)
    ]
    starts = at_index(np.asarray(table, np.int32) * count, "fcol")

    def block(which):
        return lax.dynamic_slice_in_dim(partial, starts[which], count, axis=0)

    sent = [block(2 * step + 1) for step in range(fars)]
    return sent, [block(2 * step) + swapped(sent[step], "fcol", n_fcol, 1) for step in range(fars)]


def far_sum(halves, n_fcol):
    total = halves[-1]
    for step in range(1, len(halves)):
        perm = [(i, (i + 2 * step) % n_fcol) for i in range(n_fcol)]
        total = total + lax.ppermute(halves[step - 1], "fcol", perm)
    return total


def ring_order(size):
    line = size // 2
    return [2 * z for z in range(line)] + [2 * z + 1 for z in reversed(range(line))]


def apply_sigma(sigma, own, row_block, size, n_fcol, panels):
    ring = ring_order(size)
    spot = {index: place for place, index in enumerate(ring)}

    def send(values, step):
        perm = [(ring[place], ring[(place + step) % size]) for place in range(size)]
        return lax.ppermute(values, "frow", perm)

    def owner(step):
        return [ring[(spot[index] - step) % size] for index in range(size)]

    half = own.shape[1] // 2
    held = {1: own, -1: own}
    groups = [([[own]], [owner(0)])]
    for step in range(1, size // 2):
        held = {way: send(held[way], way) for way in (1, -1)}
        groups.append(([[held[1]], [held[-1]]], [owner(step), owner(-step)]))
    parts = [send(held[-1][:, :half], -1), send(held[1][:, half:], 1)]
    groups.append(([parts], [owner(size // 2)]))
    total = None
    for items, owners in groups[:-1]:
        total = add_windows(sigma, items, list(zip(*owners)), total)[0]
    items, owners = groups[-1]
    total, inner = add_windows(sigma, items, list(zip(*owners)), total, row_block, panels)
    sent, halves = near_sums(total, n_fcol)
    applied = far_sum(halves, n_fcol)
    return applied, sum_everywhere(after(inner, *sent), applied, size, n_fcol)


def on_device(n_frow, n_fcol, sigma_anc, lower, inv_diag, sep_lower, row_pattern):
    panels = inv_diag.shape[0]
    width = inv_diag.shape[1]
    tri_inv = jnp.tril(inv_diag)
    row_mask = row_pattern.astype(jnp.float32)
    order = list(reversed(range(panels)))
    count = lower.shape[0]
    by_ring = (
        n_frow in (4, LONGEST_RING)
        and n_fcol & (n_fcol - 1) == 0
        and width % (8 * n_fcol) == 0
        and width % LANES == 0
        and sigma_anc.shape[0] % 16 == 0
        and window_plan(count, n_frow, sigma_anc.shape[1])[2]
    )
    coupled = {}
    for current in range(panels):
        for later in range(current + 1, panels):
            coupled[later, current] = matmul(
                sep_lower[
                    later * width : (later + 1) * width, current * width : (current + 1) * width
                ],
                tri_inv[current],
            )
    applied, inner_products = {}, {}
    if by_ring:
        own = all_weights(lower, inv_diag, row_pattern)
        row_block = lax.all_gather(own, "fcol", axis=0, tiled=True)
        all_applied, inner = apply_sigma(sigma_anc, own, row_block, n_frow, n_fcol, panels)
        at = 0
        for column in range(panels):
            applied[column] = all_applied[:, column * width : (column + 1) * width]
            upto = (column + 1) * width
            inner_products[column] = inner[:, at : at + upto]
            at += upto
    else:
        weighted = {}
        for column in order:
            scaled = lower[:, column * width : (column + 1) * width] * row_mask[column, 0]
            weighted[column] = matmul(scaled, tri_inv[column])
            gathered = lax.all_gather(weighted[column], "frow", axis=0, tiled=True)
            applied[column] = lax.psum_scatter(
                matmul(sigma_anc, gathered), "fcol", scatter_dimension=0, tiled=True
            )
        for column in order:
            earlier = jnp.concatenate([weighted[k] for k in range(column + 1)], axis=1)
            inner_products[column] = lax.psum(
                crossed(applied[column], earlier), ("frow", "fcol")
            )
    rows_sig, products, cross, diag = {}, {}, {}, {}

    def sep_block(first, second):
        if first == second:
            return diag[first]
        if second > first:
            return cross[second, first].T
        return cross[first, second]

    for current in order:
        block_rows = -applied[current]
        for later in range(current + 1, panels):
            block_rows = block_rows - matmul(rows_sig[later], coupled[later, current])
        rows_sig[current] = block_rows
        for column in range(current + 1):
            inner = inner_products[current][:, column * width : (column + 1) * width]
            for later in range(current + 1, panels):
                inner = inner + crossed(coupled[later, current], products[later, column])
            products[current, column] = -inner
    for current in order:
        later_set = list(range(current + 1, panels))
        for later in later_set:
            entry = -products[later, current]
            for third in later_set:
                entry = entry - matmul(sep_block(later, third), coupled[third, current])
            cross[later, current] = entry
        inner = crossed(tri_inv[current], tri_inv[current]) - products[current, current]
        for later in later_set:
            inner = inner - crossed(coupled[later, current], cross[later, current])
        diag[current] = inner
    off_rows = jnp.concatenate([rows_sig[column] for column in range(panels)], axis=1)
    sep_sigma = jnp.concatenate(
        [
            jnp.concatenate([sep_block(first, second) for second in range(panels)], axis=1)
            for first in range(panels)
        ],
        axis=0,
    )
    return off_rows, sep_sigma


def solution(mesh):
    in_specs = (P("frow", "fcol"), P(("frow", "fcol"), None), P(), P(), P(None, ("frow", "fcol")))
    out_specs = (P(("frow", "fcol"), None), P())
    return jax.shard_map(
        functools.partial(on_device, mesh.shape["frow"], mesh.shape["fcol"]),
        mesh=mesh,
        in_specs=in_specs,
        out_specs=out_specs,
        check_vma=False,
    )
```

```python
import functools
import math

import jax
import jax.numpy as jnp
import numpy as np
from jax import lax
from jax.experimental import pallas as pl
from jax.experimental.pallas import tpu as pltpu
from jax.sharding import PartitionSpec as P

LANES = 128
LONGEST_RING = 8


def matmul(left_arg, right_arg):
    return jnp.dot(
        left_arg, right_arg, precision=lax.Precision.HIGH, preferred_element_type=jnp.float32
    )


def crossed(left_arg, right_arg):
    return lax.dot_general(
        left_arg,
        right_arg,
        (((0,), (0,)), ((), ())),
        precision=lax.Precision.HIGH,
        preferred_element_type=jnp.float32,
    )


def two_parts(values):
    high = values.astype(jnp.bfloat16)
    return high, (values - high.astype(jnp.float32)).astype(jnp.bfloat16)


def product(left_parts, right_parts, dims=(((1,), (0,)), ((), ()))):
    def one(left, right):
        return lax.dot_general(left, right, dims, preferred_element_type=jnp.float32)

    (high, low), (other_high, other_low) = left_parts, right_parts
    return one(high, other_high) + one(high, other_low) + one(low, other_high)


def weights_kernel(pattern, lower, inv_diag, out):
    width = inv_diag.shape[1]
    below = lax.broadcasted_iota(jnp.int32, (width, width), 0) >= lax.broadcasted_iota(
        jnp.int32, (width, width), 1
    )
    for panel in range(inv_diag.shape[0]):
        columns = slice(panel * width, (panel + 1) * width)
        scaled = lower[:, columns] * pattern[panel, 0].astype(jnp.float32)
        tri_inv = jnp.where(below, inv_diag[panel], 0.0)
        out[:, columns] = product(two_parts(scaled), two_parts(tri_inv))


def all_weights(lower, inv_diag, row_pattern):
    return pl.pallas_call(
        weights_kernel,
        out_shape=jax.ShapeDtypeStruct(lower.shape, jnp.float32),
        in_specs=[
            pl.BlockSpec(memory_space=pltpu.SMEM),
            pl.BlockSpec(memory_space=pltpu.VMEM),
            pl.BlockSpec(memory_space=pltpu.VMEM),
        ],
        out_specs=pl.BlockSpec(memory_space=pltpu.VMEM),
        compiler_params=pltpu.CompilerParams(vmem_limit_bytes=32 * 1024 * 1024),
    )(row_pattern, lower, inv_diag)


def window_kernel(plan, places, *refs):
    windows, has_sum, with_inner, strip = plan
    refs = list(refs)
    mains = [refs.pop(0) for _ in range(windows)]
    lasts = [refs.pop(0) for _ in range(windows)]
    items = [refs.pop(0) for _ in range(windows)]
    sum_in = refs.pop(0) if has_sum else None
    row_block = refs.pop(0) if with_inner else None
    out = refs.pop(0)
    inner = refs.pop(0) if with_inner else None
    w_rows, w_high, w_low = refs
    depth = w_rows.shape[0]
    count = items[0].shape[0]

    @pl.when(pl.program_id(0) == 0)
    def _():
        for window in range(windows):
            w_rows[...] = jnp.zeros_like(w_rows)
            offset = pl.multiple_of(places[4 * window + 2], 8)
            w_rows[pl.ds(offset, count), :] = items[window][...]
            high, low = two_parts(w_rows[...])
            w_high[window * depth : (window + 1) * depth, :] = high
            w_low[window * depth : (window + 1) * depth, :] = low
        if with_inner:
            inner[...] = jnp.zeros_like(inner)

    lane = lax.broadcasted_iota(jnp.int32, (strip, LANES), 1)
    for start in range(0, out.shape[0], strip):
        rows = slice(start, start + strip)
        highs, lows = [], []
        for window in range(windows):
            last = jnp.where(lane < places[4 * window + 3], lasts[window][rows, :], 0.0)
            for values in (mains[window][rows, :], last):
                high, low = two_parts(values)
                highs.append(high)
                lows.append(low)
        high = jnp.concatenate(highs, axis=1)
        low = jnp.concatenate(lows, axis=1)
        total = product((high, low), (w_high[...], w_low[...]))
        if has_sum:
            total += sum_in[rows, :]
        out[rows, :] = total
        if with_inner:
            inner[...] += product(
                two_parts(total), two_parts(row_block[rows, :]), (((0,), (0,)), ((), ()))
            )


def row_tiles(rows):
    tiles = [tile for tile in range(16, min(rows, 640) + 1, 16) if rows % tile == 0]
    tile = max(tiles)
    return tile, tile


def window_plan(count, blocks, columns):
    main = -(-(count + 8) // LANES) * LANES
    starts = [min(count * block, columns - main) // LANES * LANES for block in range(blocks)]
    fits = all(
        count * block - start + count <= main + LANES for block, start in enumerate(starts)
    )
    return main, starts, fits and columns >= main and count % 8 == 0


def add_windows(sigma, items, owners, total, width, part=None, row_block=None):
    rows, columns = sigma.shape
    count = items[0].shape[0]
    windows = len(items)
    main, starts, _ = window_plan(count, columns // count, columns)
    depth = main + LANES
    tile, strip = row_tiles(rows)
    final = (columns - 1) // LANES
    table = []
    for blocks in owners:
        row = []
        for block in blocks:
            behind = (starts[block] + main) // LANES
            room = max(columns - behind * LANES, 0)
            row += [starts[block] // LANES, min(behind, final), count * block - starts[block], room]
        table.append(row)
    places = at_index(np.asarray(table, np.int32), "frow")

    def main_at(window):
        return lambda step, places: (
            pl.multiple_of(step * tile, tile),
            pl.multiple_of(places[4 * window] * LANES, LANES),
        )

    def last_at(window):
        return lambda step, places: (step, places[4 * window + 1])

    def by_row(step, places):
        return (step, 0)

    def whole(step, places):
        return (0, 0)

    def at_part(step, places):
        return (0, part)

    in_specs = [
        pl.BlockSpec((pl.Element(tile), pl.Element(main)), main_at(k)) for k in range(windows)
    ]
    in_specs += [pl.BlockSpec((tile, LANES), last_at(k)) for k in range(windows)]
    for item in items:
        in_specs.append(pl.BlockSpec((count, width), whole if item.shape[1] == width else at_part))
    operands = [places] + [sigma] * (2 * windows) + list(items)
    aliases = {}
    if total is not None:
        if total.shape[1] == width:
            in_specs.append(pl.BlockSpec((tile, width), by_row))
            aliases = {len(operands): 0}
        else:
            in_specs.append(pl.BlockSpec((tile, width), lambda step, places: (step, part)))
        operands.append(total)
    out_shape = [jax.ShapeDtypeStruct((rows, width), jnp.float32)]
    out_specs = [pl.BlockSpec((tile, width), by_row)]
    flops = 6 * rows * windows * depth * width
    if row_block is not None:
        inner_shape = (width, width * (part + 1))
        in_specs.append(pl.BlockSpec((tile, inner_shape[1]), by_row))
        operands.append(row_block)
        out_shape.append(jax.ShapeDtypeStruct(inner_shape, jnp.float32))
        out_specs.append(pl.BlockSpec(inner_shape, whole))
        flops += 6 * rows * inner_shape[0] * inner_shape[1]
    plan = (windows, total is not None, row_block is not None, strip)
    return pl.pallas_call(
        functools.partial(window_kernel, plan),
        out_shape=out_shape,
        grid_spec=pltpu.PrefetchScalarGridSpec(
            num_scalar_prefetch=1,
            grid=(rows // tile,),
            in_specs=in_specs,
            out_specs=out_specs,
            scratch_shapes=[
                pltpu.VMEM((depth, width), jnp.float32),
                pltpu.VMEM((windows * depth, width), jnp.bfloat16),
                pltpu.VMEM((windows * depth, width), jnp.bfloat16),
            ],
        ),
        input_output_aliases=aliases,
        compiler_params=pltpu.CompilerParams(
            dimension_semantics=("arbitrary",), vmem_limit_bytes=52 * 1024 * 1024
        ),
        cost_estimate=pl.CostEstimate(
            flops=flops, bytes_accessed=4 * rows * windows * depth, transcendentals=0
        ),
    )(*operands)


def at_index(table, axis):
    return lax.dynamic_index_in_dim(jnp.asarray(table), lax.axis_index(axis), 0, keepdims=False)


def after(values, *others):
    return lax.optimization_barrier((values,) + others)[0]


def swapped(values, axis, size, bit):
    return lax.ppermute(values, axis, [(index, index ^ bit) for index in range(size)])


def sum_near_halves(values, n_fcol):
    near = lax.axis_index("fcol") & 1
    half = values.shape[0] // 2
    kept = lax.dynamic_slice_in_dim(values, near * half, half, axis=0)
    sent = lax.dynamic_slice_in_dim(values, (1 - near) * half, half, axis=0)
    return kept + swapped(sent, "fcol", n_fcol, 1)


def sum_pairs(values, axis, size, powers):
    for power in powers:
        values = values + swapped(values, axis, size, 1 << power)
    return values


def join_near_halves(values, n_fcol):
    other = swapped(values, "fcol", n_fcol, 1)
    upper = (lax.axis_index("fcol") & 1) != 0
    return jnp.concatenate(
        [jnp.where(upper, other, values), jnp.where(upper, values, other)], axis=0
    )


def near_sums(partial, n_fcol):
    fars = n_fcol // 2
    count = partial.shape[0] // n_fcol
    table = [
        [
            (i // 2 + step) % fars * 2 + near
            for step in range(1, fars + 1)
            for near in (i % 2, 1 - i % 2)
        ]
        for i in range(n_fcol)
    ]
    starts = at_index(np.asarray(table, np.int32) * count, "fcol")

    def block(which):
        return lax.dynamic_slice_in_dim(partial, starts[which], count, axis=0)

    sent = [block(2 * step + 1) for step in range(fars)]
    return sent, [block(2 * step) + swapped(sent[step], "fcol", n_fcol, 1) for step in range(fars)]


def far_sum(halves, n_fcol):
    total = halves[-1]
    for step in range(1, len(halves)):
        perm = [(i, (i + 2 * step) % n_fcol) for i in range(n_fcol)]
        total = total + lax.ppermute(halves[step - 1], "fcol", perm)
    return total


def ring_order(size):
    line = size // 2
    return [2 * z for z in range(line)] + [2 * z + 1 for z in reversed(range(line))]


def apply_sigma(sigma, own, row_block, size, n_fcol, panels):
    ring = ring_order(size)
    spot = {index: place for place, index in enumerate(ring)}

    def send(values, step):
        perm = [(ring[place], ring[(place + step) % size]) for place in range(size)]
        return lax.ppermute(values, "frow", perm)

    def owner(step):
        return [ring[(spot[index] - step) % size] for index in range(size)]

    width = own.shape[1] // panels
    held = {1: own, -1: own}
    total = add_windows(sigma, [own], [[block] for block in owner(0)], None, own.shape[1])[0]
    for step in range(1, size // 2):
        held = {way: send(held[way], way) for way in (1, -1)}
        items = [held[1], held[-1]]
        owners = list(zip(owner(step), owner(-step)))
        if step < size // 2 - 1:
            total = add_windows(sigma, items, owners, total, own.shape[1])[0]
    order = list(reversed(range(panels)))
    far = {}
    for turn, panel in enumerate(order):
        way = 1 if turn % 2 == 0 else -1
        far[panel] = send(held[way][:, panel * width : (panel + 1) * width], way)
    applied, inner_sums = {}, {}
    frow_powers = list(range(size.bit_length() - 1))
    beside = []
    for panel in order:
        if beside:
            items = [after(items[0], *beside[0])] + items[1:]
        partial = add_windows(sigma, items, owners, total, width, panel)[0]
        item = far[panel]
        if beside:
            item = after(item, *beside[1])
        partial, inner = add_windows(
            sigma, [item], [[block] for block in owner(size // 2)], partial, width, panel, row_block
        )
        sent, halves = near_sums(partial, n_fcol)
        applied[panel] = far_sum(halves, n_fcol)
        first = sum_near_halves(after(inner, *sent), n_fcol)
        first = sum_pairs(after(first, halves[0]), "frow", size, frow_powers[:1])
        inner_sums[panel] = sum_pairs(first, "frow", size, frow_powers[1:-1])
        beside = [sent, [first] + halves]
    for panel in order:
        inner = after(inner_sums[panel], applied[panel], halves[0])
        inner = sum_pairs(inner, "frow", size, frow_powers[-1:])
        inner = sum_pairs(inner, "fcol", n_fcol, range(1, n_fcol.bit_length() - 1))
        inner_sums[panel] = join_near_halves(inner, n_fcol)
    return applied, inner_sums


def on_device(n_frow, n_fcol, sigma_anc, lower, inv_diag, sep_lower, row_pattern):
    panels = inv_diag.shape[0]
    width = inv_diag.shape[1]
    tri_inv = jnp.tril(inv_diag)
    row_mask = row_pattern.astype(jnp.float32)
    order = list(reversed(range(panels)))
    count = lower.shape[0]
    by_ring = (
        n_frow in (4, LONGEST_RING)
        and n_fcol & (n_fcol - 1) == 0
        and width % (8 * n_fcol) == 0
        and width % LANES == 0
        and sigma_anc.shape[0] % 16 == 0
        and window_plan(count, n_frow, sigma_anc.shape[1])[2]
    )
    coupled = {}
    for current in range(panels):
        for later in range(current + 1, panels):
            coupled[later, current] = matmul(
                sep_lower[
                    later * width : (later + 1) * width, current * width : (current + 1) * width
                ],
                tri_inv[current],
            )
    applied, inner_products = {}, {}
    if by_ring:
        own = all_weights(lower, inv_diag, row_pattern)
        row_block = lax.all_gather(own, "fcol", axis=0, tiled=True)
        applied, inner_products = apply_sigma(
            sigma_anc, own, row_block, n_frow, n_fcol, panels
        )
    else:
        weighted = {}
        for column in order:
            scaled = lower[:, column * width : (column + 1) * width] * row_mask[column, 0]
            weighted[column] = matmul(scaled, tri_inv[column])
            gathered = lax.all_gather(weighted[column], "frow", axis=0, tiled=True)
            applied[column] = lax.psum_scatter(
                matmul(sigma_anc, gathered), "fcol", scatter_dimension=0, tiled=True
            )
        for column in order:
            earlier = jnp.concatenate([weighted[k] for k in range(column + 1)], axis=1)
            inner_products[column] = lax.psum(
                crossed(applied[column], earlier), ("frow", "fcol")
            )
    rows_sig, products, cross, diag = {}, {}, {}, {}

    def sep_block(first, second):
        if first == second:
            return diag[first]
        if second > first:
            return cross[second, first].T
        return cross[first, second]

    for current in order:
        block_rows = -applied[current]
        for later in range(current + 1, panels):
            block_rows = block_rows - matmul(rows_sig[later], coupled[later, current])
        rows_sig[current] = block_rows
        for column in range(current + 1):
            inner = inner_products[current][:, column * width : (column + 1) * width]
            for later in range(current + 1, panels):
                inner = inner + crossed(coupled[later, current], products[later, column])
            products[current, column] = -inner
    for current in order:
        later_set = list(range(current + 1, panels))
        for later in later_set:
            entry = -products[later, current]
            for third in later_set:
                entry = entry - matmul(sep_block(later, third), coupled[third, current])
            cross[later, current] = entry
        inner = crossed(tri_inv[current], tri_inv[current]) - products[current, current]
        for later in later_set:
            inner = inner - crossed(coupled[later, current], cross[later, current])
        diag[current] = inner
    off_rows = jnp.concatenate([rows_sig[column] for column in range(panels)], axis=1)
    sep_sigma = jnp.concatenate(
        [
            jnp.concatenate([sep_block(first, second) for second in range(panels)], axis=1)
            for first in range(panels)
        ],
        axis=0,
    )
    return off_rows, sep_sigma


def solution(mesh):
    in_specs = (P("frow", "fcol"), P(("frow", "fcol"), None), P(), P(), P(None, ("frow", "fcol")))
    out_specs = (P(("frow", "fcol"), None), P())
    return jax.shard_map(
        functools.partial(on_device, mesh.shape["frow"], mesh.shape["fcol"]),
        mesh=mesh,
        in_specs=in_specs,
        out_specs=out_specs,
        check_vma=False,
    )
```

```python
import functools
import math

import jax
import jax.numpy as jnp
import numpy as np
from jax import lax
from jax.experimental import pallas as pl
from jax.experimental.pallas import tpu as pltpu
from jax.sharding import PartitionSpec as P

LANES = 128
LONGEST_RING = 8


def matmul(left_arg, right_arg):
    return jnp.dot(
        left_arg, right_arg, precision=lax.Precision.HIGH, preferred_element_type=jnp.float32
    )


def crossed(left_arg, right_arg):
    return lax.dot_general(
        left_arg,
        right_arg,
        (((0,), (0,)), ((), ())),
        precision=lax.Precision.HIGH,
        preferred_element_type=jnp.float32,
    )


def two_parts(values):
    high = values.astype(jnp.bfloat16)
    return high, (values - high.astype(jnp.float32)).astype(jnp.bfloat16)


def product(left_parts, right_parts, dims=(((1,), (0,)), ((), ()))):
    def one(left, right):
        return lax.dot_general(left, right, dims, preferred_element_type=jnp.float32)

    (high, low), (other_high, other_low) = left_parts, right_parts
    return one(high, other_high) + one(high, other_low) + one(low, other_high)


def weights_kernel(pattern, lower, inv_diag, out):
    width = inv_diag.shape[1]
    below = lax.broadcasted_iota(jnp.int32, (width, width), 0) >= lax.broadcasted_iota(
        jnp.int32, (width, width), 1
    )
    for panel in range(inv_diag.shape[0]):
        columns = slice(panel * width, (panel + 1) * width)
        scaled = lower[:, columns] * pattern[panel, 0].astype(jnp.float32)
        tri_inv = jnp.where(below, inv_diag[panel], 0.0)
        out[:, columns] = product(two_parts(scaled), two_parts(tri_inv))


def all_weights(lower, inv_diag, row_pattern):
    return pl.pallas_call(
        weights_kernel,
        out_shape=jax.ShapeDtypeStruct(lower.shape, jnp.float32),
        in_specs=[
            pl.BlockSpec(memory_space=pltpu.SMEM),
            pl.BlockSpec(memory_space=pltpu.VMEM),
            pl.BlockSpec(memory_space=pltpu.VMEM),
        ],
        out_specs=pl.BlockSpec(memory_space=pltpu.VMEM),
        compiler_params=pltpu.CompilerParams(vmem_limit_bytes=32 * 1024 * 1024),
    )(row_pattern, lower, inv_diag)


def window_kernel(plan, places, *refs):
    windows, parts, has_sum, with_inner, panels, strip = plan
    refs = list(refs)
    mains = [refs.pop(0) for _ in range(windows)]
    lasts = [refs.pop(0) for _ in range(windows)]
    items = [[refs.pop(0) for _ in range(parts)] for _ in range(windows)]
    sum_in = refs.pop(0) if has_sum else None
    row_block = refs.pop(0) if with_inner else None
    out = refs.pop(0)
    inner = refs.pop(0) if with_inner else None
    w_rows, w_high, w_low = refs
    depth = w_rows.shape[0]
    count, part_width = items[0][0].shape

    @pl.when(pl.program_id(0) == 0)
    def _():
        for window in range(windows):
            w_rows[...] = jnp.zeros_like(w_rows)
            offset = pl.multiple_of(places[4 * window + 2], 8)
            for part in range(parts):
                columns = slice(part * part_width, (part + 1) * part_width)
                w_rows[pl.ds(offset, count), columns] = items[window][part][...]
            high, low = two_parts(w_rows[...])
            w_high[window * depth : (window + 1) * depth, :] = high
            w_low[window * depth : (window + 1) * depth, :] = low
        if with_inner:
            inner[...] = jnp.zeros_like(inner)

    lane = lax.broadcasted_iota(jnp.int32, (strip, LANES), 1)
    for start in range(0, out.shape[0], strip):
        rows = slice(start, start + strip)
        highs, lows = [], []
        for window in range(windows):
            last = jnp.where(lane < places[4 * window + 3], lasts[window][rows, :], 0.0)
            for values in (mains[window][rows, :], last):
                high, low = two_parts(values)
                highs.append(high)
                lows.append(low)
        high = jnp.concatenate(highs, axis=1)
        low = jnp.concatenate(lows, axis=1)
        total = product((high, low), (w_high[...], w_low[...]))
        if has_sum:
            total += sum_in[rows, :]
        out[rows, :] = total
        if with_inner:
            width = total.shape[1] // panels
            others = two_parts(row_block[rows, :])
            at = 0
            for panel in range(panels):
                mine = two_parts(total[:, panel * width : (panel + 1) * width])
                upto = (panel + 1) * width
                inner[:, at : at + upto] += product(
                    mine, [other[:, :upto] for other in others], (((0,), (0,)), ((), ()))
                )
                at += upto


def row_tiles(rows):
    tiles = [tile for tile in range(16, min(rows, 640) + 1, 16) if rows % tile == 0]
    tile = max(tiles)
    strips = [strip for strip in range(16, min(tile, 256) + 1, 16) if tile % strip == 0]
    return tile, max(strips)


def window_plan(count, blocks, columns):
    main = -(-(count + 8) // LANES) * LANES
    starts = [min(count * block, columns - main) // LANES * LANES for block in range(blocks)]
    fits = all(
        count * block - start + count <= main + LANES for block, start in enumerate(starts)
    )
    return main, starts, fits and columns >= main and count % 8 == 0


def add_windows(sigma, items, owners, total, row_block=None, panels=1, half=None):
    all_rows, columns = sigma.shape
    rows = all_rows if half is None else all_rows // 2
    count = items[0][0].shape[0]
    parts = len(items[0])
    width = parts * items[0][0].shape[1]
    windows = len(items)
    main, starts, _ = window_plan(count, columns // count, columns)
    depth = main + LANES
    tile, strip = row_tiles(rows)
    final = (columns - 1) // LANES
    table = []
    for blocks in owners:
        row = []
        for block in blocks:
            behind = (starts[block] + main) // LANES
            room = max(columns - behind * LANES, 0)
            row += [starts[block] // LANES, min(behind, final), count * block - starts[block], room]
        table.append(row)
    places = at_index(np.asarray(table, np.int32), "frow")
    first = 0 if half is None else half * (rows // tile)
    places = jnp.concatenate([places, jnp.asarray(first, jnp.int32).reshape(1)])
    first_at = 4 * windows

    def main_at(window):
        return lambda step, places: (
            pl.multiple_of((places[first_at] + step) * tile, tile),
            pl.multiple_of(places[4 * window] * LANES, LANES),
        )

    def last_at(window):
        return lambda step, places: (places[first_at] + step, places[4 * window + 1])

    def by_row(step, places):
        return (step, 0)

    def by_all_rows(step, places):
        return (places[first_at] + step, 0)

    def whole(step, places):
        return (0, 0)

    in_specs = [
        pl.BlockSpec((pl.Element(tile), pl.Element(main)), main_at(k)) for k in range(windows)
    ]
    in_specs += [pl.BlockSpec((tile, LANES), last_at(k)) for k in range(windows)]
    in_specs += [pl.BlockSpec((count, width // parts), whole)] * (windows * parts)
    operands = [places] + [sigma] * (2 * windows) + [part for item in items for part in item]
    aliases = {}
    if total is not None:
        if total.shape[0] == rows:
            in_specs.append(pl.BlockSpec((tile, width), by_row))
            aliases = {len(operands): 0}
        else:
            in_specs.append(pl.BlockSpec((tile, width), by_all_rows))
        operands.append(total)
    out_shape = [jax.ShapeDtypeStruct((rows, width), jnp.float32)]
    out_specs = [pl.BlockSpec((tile, width), by_row)]
    flops = 6 * rows * windows * depth * width
    if row_block is not None:
        in_specs.append(pl.BlockSpec((tile, width), by_all_rows))
        operands.append(row_block)
        panel_width = width // panels
        inner_shape = (panel_width, panel_width * panels * (panels + 1) // 2)
        out_shape.append(jax.ShapeDtypeStruct(inner_shape, jnp.float32))
        out_specs.append(pl.BlockSpec(inner_shape, whole))
        flops += 6 * rows * inner_shape[0] * inner_shape[1]
    plan = (windows, parts, total is not None, row_block is not None, panels, strip)
    return pl.pallas_call(
        functools.partial(window_kernel, plan),
        out_shape=out_shape,
        grid_spec=pltpu.PrefetchScalarGridSpec(
            num_scalar_prefetch=1,
            grid=(rows // tile,),
            in_specs=in_specs,
            out_specs=out_specs,
            scratch_shapes=[
                pltpu.VMEM((depth, width), jnp.float32),
                pltpu.VMEM((windows * depth, width), jnp.bfloat16),
                pltpu.VMEM((windows * depth, width), jnp.bfloat16),
            ],
        ),
        input_output_aliases=aliases,
        compiler_params=pltpu.CompilerParams(
            dimension_semantics=("arbitrary",), vmem_limit_bytes=52 * 1024 * 1024
        ),
        cost_estimate=pl.CostEstimate(
            flops=flops, bytes_accessed=4 * rows * windows * depth, transcendentals=0
        ),
    )(*operands)


def at_index(table, axis):
    return lax.dynamic_index_in_dim(jnp.asarray(table), lax.axis_index(axis), 0, keepdims=False)


def after(values, *others):
    return lax.optimization_barrier((values,) + others)[0]


def swapped(values, axis, size, bit):
    return lax.ppermute(values, axis, [(index, index ^ bit) for index in range(size)])


def sum_everywhere(values, beside, n_frow, n_fcol):
    bits = [1 << power for power in range(n_fcol.bit_length() - 1)]
    index = lax.axis_index("fcol")
    for bit in bits:
        half = values.shape[0] // 2
        mine = ((index & bit) != 0).astype(jnp.int32)
        kept = lax.dynamic_slice_in_dim(values, mine * half, half, axis=0)
        sent = lax.dynamic_slice_in_dim(values, (1 - mine) * half, half, axis=0)
        values = kept + swapped(sent, "fcol", n_fcol, bit)
    for power in range(n_frow.bit_length() - 1):
        values = values + swapped(values, "frow", n_frow, 1 << power)
    values = after(values, beside)
    for bit in reversed(bits):
        other = swapped(values, "fcol", n_fcol, bit)
        upper = (index & bit) != 0
        values = jnp.concatenate(
            [jnp.where(upper, other, values), jnp.where(upper, values, other)], axis=0
        )
    return values


def near_sum(partial, n_fcol):
    near = lax.axis_index("fcol") & 1
    count = partial.shape[0] // 2
    kept = lax.dynamic_slice_in_dim(partial, near * count, count, axis=0)
    sent = lax.dynamic_slice_in_dim(partial, (1 - near) * count, count, axis=0)
    return kept + swapped(sent, "fcol", n_fcol, 1)


def ring_order(size):
    line = size // 2
    return [2 * z for z in range(line)] + [2 * z + 1 for z in reversed(range(line))]


def apply_sigma(sigma, own, row_block, size, n_fcol, panels):
    ring = ring_order(size)
    spot = {index: place for place, index in enumerate(ring)}

    def send(values, step):
        perm = [(ring[place], ring[(place + step) % size]) for place in range(size)]
        return lax.ppermute(values, "frow", perm)

    def owner(step):
        return [ring[(spot[index] - step) % size] for index in range(size)]

    half = own.shape[1] // 2
    held = {1: own, -1: own}
    groups = [([[own]], [owner(0)])]
    for step in range(1, size // 2):
        held = {way: send(held[way], way) for way in (1, -1)}
        groups.append(([[held[1]], [held[-1]]], [owner(step), owner(-step)]))
    parts = [send(held[-1][:, :half], -1), send(held[1][:, half:], 1)]
    groups.append(([parts], [owner(size // 2)]))
    total = None
    for items, owners in groups[:-2]:
        total = add_windows(sigma, items, list(zip(*owners)), total)[0]
    far = lax.axis_index("fcol") >> 1
    (pair, pair_owners), (last, last_owners) = groups[-2:]
    def rows_done(half, pair, last):
        partial = add_windows(sigma, pair, list(zip(*pair_owners)), total, half=half)[0]
        owners = list(zip(*last_owners))
        return add_windows(sigma, last(), owners, partial, row_block, panels, half)

    partial, inner = rows_done(1 - far, pair, lambda: last)
    away = near_sum(partial, n_fcol)
    cut = away.shape[1] // 2
    come_first = swapped(away[:, :cut], "fcol", n_fcol, 2)
    come_next = swapped(after(away[:, cut:], come_first), "fcol", n_fcol, 2)
    pair = [[after(pair[0][0], away)], pair[1]]
    partial, other_inner = rows_done(
        far, pair, lambda: [[after(last[0][0], come_first, inner)] + last[0][1:]]
    )
    applied = near_sum(partial, n_fcol) + jnp.concatenate([come_first, come_next], axis=1)
    inner = after(inner + other_inner, come_next)
    return applied, sum_everywhere(inner, applied, size, n_fcol)


def on_device(n_frow, n_fcol, sigma_anc, lower, inv_diag, sep_lower, row_pattern):
    panels = inv_diag.shape[0]
    width = inv_diag.shape[1]
    tri_inv = jnp.tril(inv_diag)
    row_mask = row_pattern.astype(jnp.float32)
    order = list(reversed(range(panels)))
    count = lower.shape[0]
    by_ring = (
        n_frow in (4, LONGEST_RING)
        and n_fcol == 4
        and width % (8 * n_fcol) == 0
        and width % LANES == 0
        and sigma_anc.shape[0] % 32 == 0
        and window_plan(count, n_frow, sigma_anc.shape[1])[2]
    )
    coupled = {}
    for current in range(panels):
        for later in range(current + 1, panels):
            coupled[later, current] = matmul(
                sep_lower[
                    later * width : (later + 1) * width, current * width : (current + 1) * width
                ],
                tri_inv[current],
            )
    applied, inner_products = {}, {}
    if by_ring:
        own = all_weights(lower, inv_diag, row_pattern)
        row_block = lax.all_gather(own, "fcol", axis=0, tiled=True)
        all_applied, inner = apply_sigma(sigma_anc, own, row_block, n_frow, n_fcol, panels)
        at = 0
        for column in range(panels):
            applied[column] = all_applied[:, column * width : (column + 1) * width]
            upto = (column + 1) * width
            inner_products[column] = inner[:, at : at + upto]
            at += upto
    else:
        weighted = {}
        for column in order:
            scaled = lower[:, column * width : (column + 1) * width] * row_mask[column, 0]
            weighted[column] = matmul(scaled, tri_inv[column])
            gathered = lax.all_gather(weighted[column], "frow", axis=0, tiled=True)
            applied[column] = lax.psum_scatter(
                matmul(sigma_anc, gathered), "fcol", scatter_dimension=0, tiled=True
            )
        for column in order:
            earlier = jnp.concatenate([weighted[k] for k in range(column + 1)], axis=1)
            inner_products[column] = lax.psum(
                crossed(applied[column], earlier), ("frow", "fcol")
            )
    rows_sig, products, cross, diag = {}, {}, {}, {}

    def sep_block(first, second):
        if first == second:
            return diag[first]
        if second > first:
            return cross[second, first].T
        return cross[first, second]

    for current in order:
        block_rows = -applied[current]
        for later in range(current + 1, panels):
            block_rows = block_rows - matmul(rows_sig[later], coupled[later, current])
        rows_sig[current] = block_rows
        for column in range(current + 1):
            inner = inner_products[current][:, column * width : (column + 1) * width]
            for later in range(current + 1, panels):
                inner = inner + crossed(coupled[later, current], products[later, column])
            products[current, column] = -inner
    for current in order:
        later_set = list(range(current + 1, panels))
        for later in later_set:
            entry = -products[later, current]
            for third in later_set:
                entry = entry - matmul(sep_block(later, third), coupled[third, current])
            cross[later, current] = entry
        inner = crossed(tri_inv[current], tri_inv[current]) - products[current, current]
        for later in later_set:
            inner = inner - crossed(coupled[later, current], cross[later, current])
        diag[current] = inner
    off_rows = jnp.concatenate([rows_sig[column] for column in range(panels)], axis=1)
    sep_sigma = jnp.concatenate(
        [
            jnp.concatenate([sep_block(first, second) for second in range(panels)], axis=1)
            for first in range(panels)
        ],
        axis=0,
    )
    return off_rows, sep_sigma


def solution(mesh):
    in_specs = (P("frow", "fcol"), P(("frow", "fcol"), None), P(), P(), P(None, ("frow", "fcol")))
    out_specs = (P(("frow", "fcol"), None), P())
    return jax.shard_map(
        functools.partial(on_device, mesh.shape["frow"], mesh.shape["fcol"]),
        mesh=mesh,
        in_specs=in_specs,
        out_specs=out_specs,
        check_vma=False,
    )
```

```python
import functools
import math

import jax
import jax.numpy as jnp
import numpy as np
from jax import lax
from jax.experimental import pallas as pl
from jax.experimental.pallas import tpu as pltpu
from jax.sharding import PartitionSpec as P

LANES = 128
LONGEST_RING = 8


def matmul(left_arg, right_arg):
    return jnp.dot(
        left_arg, right_arg, precision=lax.Precision.HIGH, preferred_element_type=jnp.float32
    )


def crossed(left_arg, right_arg):
    return lax.dot_general(
        left_arg,
        right_arg,
        (((0,), (0,)), ((), ())),
        precision=lax.Precision.HIGH,
        preferred_element_type=jnp.float32,
    )


def two_parts(values):
    high = values.astype(jnp.bfloat16)
    return high, (values - high.astype(jnp.float32)).astype(jnp.bfloat16)


def product(left_parts, right_parts, dims=(((1,), (0,)), ((), ()))):
    def one(left, right):
        return lax.dot_general(left, right, dims, preferred_element_type=jnp.float32)

    (high, low), (other_high, other_low) = left_parts, right_parts
    return one(high, other_high) + one(high, other_low) + one(low, other_high)


def weights_kernel(pattern, lower, inv_diag, out):
    width = inv_diag.shape[1]
    below = lax.broadcasted_iota(jnp.int32, (width, width), 0) >= lax.broadcasted_iota(
        jnp.int32, (width, width), 1
    )
    for panel in range(inv_diag.shape[0]):
        columns = slice(panel * width, (panel + 1) * width)
        scaled = lower[:, columns] * pattern[panel, 0].astype(jnp.float32)
        tri_inv = jnp.where(below, inv_diag[panel], 0.0)
        out[:, columns] = product(two_parts(scaled), two_parts(tri_inv))


def all_weights(lower, inv_diag, row_pattern):
    return pl.pallas_call(
        weights_kernel,
        out_shape=jax.ShapeDtypeStruct(lower.shape, jnp.float32),
        in_specs=[
            pl.BlockSpec(memory_space=pltpu.SMEM),
            pl.BlockSpec(memory_space=pltpu.VMEM),
            pl.BlockSpec(memory_space=pltpu.VMEM),
        ],
        out_specs=pl.BlockSpec(memory_space=pltpu.VMEM),
        compiler_params=pltpu.CompilerParams(vmem_limit_bytes=32 * 1024 * 1024),
    )(row_pattern, lower, inv_diag)


def window_kernel(plan, places, *refs):
    windows, parts, has_sum, with_inner, panels, strip = plan
    refs = list(refs)
    mains = [refs.pop(0) for _ in range(windows)]
    lasts = [refs.pop(0) for _ in range(windows)]
    items = [[refs.pop(0) for _ in range(parts[window])] for window in range(windows)]
    sum_in = refs.pop(0) if has_sum else None
    row_block = refs.pop(0) if with_inner else None
    out = refs.pop(0)
    inner = refs.pop(0) if with_inner else None
    w_rows, w_high, w_low = refs
    depth = w_rows.shape[0]
    count = items[0][0].shape[0]

    @pl.when(pl.program_id(0) == 0)
    def _():
        for window in range(windows):
            w_rows[...] = jnp.zeros_like(w_rows)
            offset = pl.multiple_of(places[4 * window + 2], 8)
            at = 0
            for part in items[window]:
                columns = slice(at, at + part.shape[1])
                w_rows[pl.ds(offset, count), columns] = part[...]
                at += part.shape[1]
            high, low = two_parts(w_rows[...])
            w_high[window * depth : (window + 1) * depth, :] = high
            w_low[window * depth : (window + 1) * depth, :] = low
        if with_inner:
            inner[...] = jnp.zeros_like(inner)

    lane = lax.broadcasted_iota(jnp.int32, (strip, LANES), 1)
    for start in range(0, out.shape[0], strip):
        rows = slice(start, start + strip)
        highs, lows = [], []
        for window in range(windows):
            last = jnp.where(lane < places[4 * window + 3], lasts[window][rows, :], 0.0)
            for values in (mains[window][rows, :], last):
                high, low = two_parts(values)
                highs.append(high)
                lows.append(low)
        high = jnp.concatenate(highs, axis=1)
        low = jnp.concatenate(lows, axis=1)
        total = product((high, low), (w_high[...], w_low[...]))
        if has_sum:
            total += sum_in[rows, :]
        out[rows, :] = total
        if with_inner:
            width = total.shape[1] // panels
            others = two_parts(row_block[rows, :])
            at = 0
            for panel in range(panels):
                mine = two_parts(total[:, panel * width : (panel + 1) * width])
                upto = (panel + 1) * width
                inner[:, at : at + upto] += product(
                    mine, [other[:, :upto] for other in others], (((0,), (0,)), ((), ()))
                )
                at += upto


def row_tiles(rows):
    tiles = [tile for tile in range(16, min(rows, 640) + 1, 16) if rows % tile == 0]
    tile = max(tiles)
    strips = [strip for strip in range(16, min(tile, 256) + 1, 16) if tile % strip == 0]
    return tile, max(strips)


def window_plan(count, blocks, columns):
    main = -(-(count + 8) // LANES) * LANES
    starts = [min(count * block, columns - main) // LANES * LANES for block in range(blocks)]
    fits = all(
        count * block - start + count <= main + LANES for block, start in enumerate(starts)
    )
    return main, starts, fits and columns >= main and count % 8 == 0


def add_windows(sigma, items, owners, total, row_block=None, panels=1, half=None):
    all_rows, columns = sigma.shape
    rows = all_rows if half is None else all_rows // 2
    count = items[0][0].shape[0]
    parts = tuple(len(item) for item in items)
    width = sum(part.shape[1] for part in items[0])
    windows = len(items)
    main, starts, _ = window_plan(count, columns // count, columns)
    depth = main + LANES
    tile, strip = row_tiles(rows)
    final = (columns - 1) // LANES
    table = []
    for blocks in owners:
        row = []
        for block in blocks:
            behind = (starts[block] + main) // LANES
            room = max(columns - behind * LANES, 0)
            row += [starts[block] // LANES, min(behind, final), count * block - starts[block], room]
        table.append(row)
    places = at_index(np.asarray(table, np.int32), "frow")
    first = 0 if half is None else half * (rows // tile)
    places = jnp.concatenate([places, jnp.asarray(first, jnp.int32).reshape(1)])
    first_at = 4 * windows

    def main_at(window):
        return lambda step, places: (
            pl.multiple_of((places[first_at] + step) * tile, tile),
            pl.multiple_of(places[4 * window] * LANES, LANES),
        )

    def last_at(window):
        return lambda step, places: (places[first_at] + step, places[4 * window + 1])

    def by_row(step, places):
        return (step, 0)

    def by_all_rows(step, places):
        return (places[first_at] + step, 0)

    def whole(step, places):
        return (0, 0)

    in_specs = [
        pl.BlockSpec((pl.Element(tile), pl.Element(main)), main_at(k)) for k in range(windows)
    ]
    in_specs += [pl.BlockSpec((tile, LANES), last_at(k)) for k in range(windows)]
    in_specs += [pl.BlockSpec(part.shape, whole) for item in items for part in item]
    operands = [places] + [sigma] * (2 * windows) + [part for item in items for part in item]
    aliases = {}
    if total is not None:
        if total.shape[0] == rows:
            in_specs.append(pl.BlockSpec((tile, width), by_row))
            aliases = {len(operands): 0}
        else:
            in_specs.append(pl.BlockSpec((tile, width), by_all_rows))
        operands.append(total)
    out_shape = [jax.ShapeDtypeStruct((rows, width), jnp.float32)]
    out_specs = [pl.BlockSpec((tile, width), by_row)]
    flops = 6 * rows * windows * depth * width
    if row_block is not None:
        in_specs.append(pl.BlockSpec((tile, width), by_all_rows))
        operands.append(row_block)
        panel_width = width // panels
        inner_shape = (panel_width, panel_width * panels * (panels + 1) // 2)
        out_shape.append(jax.ShapeDtypeStruct(inner_shape, jnp.float32))
        out_specs.append(pl.BlockSpec(inner_shape, whole))
        flops += 6 * rows * inner_shape[0] * inner_shape[1]
    plan = (windows, parts, total is not None, row_block is not None, panels, strip)
    return pl.pallas_call(
        functools.partial(window_kernel, plan),
        out_shape=out_shape,
        grid_spec=pltpu.PrefetchScalarGridSpec(
            num_scalar_prefetch=1,
            grid=(rows // tile,),
            in_specs=in_specs,
            out_specs=out_specs,
            scratch_shapes=[
                pltpu.VMEM((depth, width), jnp.float32),
                pltpu.VMEM((windows * depth, width), jnp.bfloat16),
                pltpu.VMEM((windows * depth, width), jnp.bfloat16),
            ],
        ),
        input_output_aliases=aliases,
        compiler_params=pltpu.CompilerParams(
            dimension_semantics=("arbitrary",), vmem_limit_bytes=56 * 1024 * 1024
        ),
        cost_estimate=pl.CostEstimate(
            flops=flops, bytes_accessed=4 * rows * windows * depth, transcendentals=0
        ),
    )(*operands)


def at_index(table, axis):
    return lax.dynamic_index_in_dim(jnp.asarray(table), lax.axis_index(axis), 0, keepdims=False)


def after(values, *others):
    return lax.optimization_barrier((values,) + others)[0]


def swapped(values, axis, size, bit):
    return lax.ppermute(values, axis, [(index, index ^ bit) for index in range(size)])


def sum_everywhere(values, come, beside, n_frow, n_fcol):
    bits = [1 << power for power in range(n_fcol.bit_length() - 1)]
    index = lax.axis_index("fcol")
    for bit in bits:
        half = values.shape[0] // 2
        mine = ((index & bit) != 0).astype(jnp.int32)
        kept = lax.dynamic_slice_in_dim(values, mine * half, half, axis=0)
        sent = lax.dynamic_slice_in_dim(values, (1 - mine) * half, half, axis=0)
        values = kept + swapped(sent, "fcol", n_fcol, bit)
        if bit == 1:
            applied = beside(values)
            values = after(values, come)
    for power in range(n_frow.bit_length() - 1):
        values = values + swapped(values, "frow", n_frow, 1 << power)
    values = after(values, applied)
    for bit in reversed(bits):
        other = swapped(values, "fcol", n_fcol, bit)
        upper = (index & bit) != 0
        values = jnp.concatenate(
            [jnp.where(upper, other, values), jnp.where(upper, values, other)], axis=0
        )
    return applied, values


def near_sum(partial, n_fcol):
    near = lax.axis_index("fcol") & 1
    count = partial.shape[0] // 2
    kept = lax.dynamic_slice_in_dim(partial, near * count, count, axis=0)
    sent = lax.dynamic_slice_in_dim(partial, (1 - near) * count, count, axis=0)
    return kept + swapped(sent, "fcol", n_fcol, 1)


def ring_order(size):
    line = size // 2
    return [2 * z for z in range(line)] + [2 * z + 1 for z in reversed(range(line))]


def apply_sigma(sigma, own, row_block, size, n_fcol, panels):
    ring = ring_order(size)
    spot = {index: place for place, index in enumerate(ring)}

    def send(values, step):
        perm = [(ring[place], ring[(place + step) % size]) for place in range(size)]
        return lax.ppermute(values, "frow", perm)

    def owner(step):
        return [ring[(spot[index] - step) % size] for index in range(size)]

    half = own.shape[1] // 2
    held = {1: own, -1: own}
    groups = [([[own]], [owner(0)])]
    for step in range(1, size // 2):
        held = {way: send(held[way], way) for way in (1, -1)}
        groups.append(([[held[1]], [held[-1]]], [owner(step), owner(-step)]))
    parts = [send(held[-1][:, :half], -1), send(held[1][:, half:], 1)]
    groups.append(([parts], [owner(size // 2)]))
    total = None
    for items, owners in groups[:-2]:
        total = add_windows(sigma, items, list(zip(*owners)), total)[0]
    far = lax.axis_index("fcol") >> 1
    (pair, pair_owners), (last, last_owners) = groups[-2:]
    partial = add_windows(sigma, pair, list(zip(*pair_owners)), total, half=1 - far)[0]
    partial, inner = add_windows(
        sigma, last, list(zip(*last_owners)), partial, row_block, panels, 1 - far
    )
    away = near_sum(partial, n_fcol)
    come = swapped(away, "fcol", n_fcol, 2)
    items = [[after(pair[0][0], away, inner)], pair[1]] + last
    owners = list(zip(*(pair_owners + last_owners)))
    partial, other_inner = add_windows(sigma, items, owners, total, row_block, panels, far)
    inner = inner + other_inner
    return sum_everywhere(
        inner, come, lambda first: near_sum(after(partial, first), n_fcol) + come, size, n_fcol
    )


def on_device(n_frow, n_fcol, sigma_anc, lower, inv_diag, sep_lower, row_pattern):
    panels = inv_diag.shape[0]
    width = inv_diag.shape[1]
    tri_inv = jnp.tril(inv_diag)
    row_mask = row_pattern.astype(jnp.float32)
    order = list(reversed(range(panels)))
    count = lower.shape[0]
    by_ring = (
        n_frow in (4, LONGEST_RING)
        and n_fcol == 4
        and width % (8 * n_fcol) == 0
        and width % LANES == 0
        and sigma_anc.shape[0] % 32 == 0
        and window_plan(count, n_frow, sigma_anc.shape[1])[2]
    )
    coupled = {}
    for current in range(panels):
        for later in range(current + 1, panels):
            coupled[later, current] = matmul(
                sep_lower[
                    later * width : (later + 1) * width, current * width : (current + 1) * width
                ],
                tri_inv[current],
            )
    applied, inner_products = {}, {}
    if by_ring:
        own = all_weights(lower, inv_diag, row_pattern)
        row_block = lax.all_gather(own, "fcol", axis=0, tiled=True)
        all_applied, inner = apply_sigma(sigma_anc, own, row_block, n_frow, n_fcol, panels)
        at = 0
        for column in range(panels):
            applied[column] = all_applied[:, column * width : (column + 1) * width]
            upto = (column + 1) * width
            inner_products[column] = inner[:, at : at + upto]
            at += upto
    else:
        weighted = {}
        for column in order:
            scaled = lower[:, column * width : (column + 1) * width] * row_mask[column, 0]
            weighted[column] = matmul(scaled, tri_inv[column])
            gathered = lax.all_gather(weighted[column], "frow", axis=0, tiled=True)
            applied[column] = lax.psum_scatter(
                matmul(sigma_anc, gathered), "fcol", scatter_dimension=0, tiled=True
            )
        for column in order:
            earlier = jnp.concatenate([weighted[k] for k in range(column + 1)], axis=1)
            inner_products[column] = lax.psum(
                crossed(applied[column], earlier), ("frow", "fcol")
            )
    rows_sig, products, cross, diag = {}, {}, {}, {}

    def sep_block(first, second):
        if first == second:
            return diag[first]
        if second > first:
            return cross[second, first].T
        return cross[first, second]

    for current in order:
        block_rows = -applied[current]
        for later in range(current + 1, panels):
            block_rows = block_rows - matmul(rows_sig[later], coupled[later, current])
        rows_sig[current] = block_rows
        for column in range(current + 1):
            inner = inner_products[current][:, column * width : (column + 1) * width]
            for later in range(current + 1, panels):
                inner = inner + crossed(coupled[later, current], products[later, column])
            products[current, column] = -inner
    for current in order:
        later_set = list(range(current + 1, panels))
        for later in later_set:
            entry = -products[later, current]
            for third in later_set:
                entry = entry - matmul(sep_block(later, third), coupled[third, current])
            cross[later, current] = entry
        inner = crossed(tri_inv[current], tri_inv[current]) - products[current, current]
        for later in later_set:
            inner = inner - crossed(coupled[later, current], cross[later, current])
        diag[current] = inner
    off_rows = jnp.concatenate([rows_sig[column] for column in range(panels)], axis=1)
    sep_sigma = jnp.concatenate(
        [
            jnp.concatenate([sep_block(first, second) for second in range(panels)], axis=1)
            for first in range(panels)
        ],
        axis=0,
    )
    return off_rows, sep_sigma


def solution(mesh):
    in_specs = (P("frow", "fcol"), P(("frow", "fcol"), None), P(), P(), P(None, ("frow", "fcol")))
    out_specs = (P(("frow", "fcol"), None), P())
    return jax.shard_map(
        functools.partial(on_device, mesh.shape["frow"], mesh.shape["fcol"]),
        mesh=mesh,
        in_specs=in_specs,
        out_specs=out_specs,
        check_vma=False,
    )
```
